32 devices in a mesh: seq: 16 (over z, y, core), head: 2 (over x).
Axes of the slice: x: 2, y: 2, z: 4, core: 2. Of those that a mesh axis runs over, the one named last changes fastest.
Arguments:
- target: bfloat16 [4096, 2048], P('seq', 'head'), may hold values from -1000 to 1000, as said below
- source: bfloat16 [4096, 2048], P('seq', 'head'), may hold values from -6 to 6
- w_query: bfloat16 [2048, 2048], P('seq', 'head'), may hold values from -0.125 to 0.125
- w_key: bfloat16 [2048, 2048], P('seq', 'head'), may hold values from -0.125 to 0.125
- w_value: bfloat16 [2048, 2048], P('seq', 'head'), may hold values from -0.125 to 0.125
- w_out: bfloat16 [2048, 2048], P('seq', 'head'), may hold values from -0.125 to 0.125
- band_start: int32 [64], P('seq'), may hold values from 0 to 63, as said below
- band_end: int32 [64], P('seq'), may hold values from 1 to 64, as said below
- cotangent: bfloat16 [4096, 2048], P('seq', 'head'), may hold values from -6 to 6
Outputs:
- attended: bfloat16 [4096, 2048], P('seq', 'head')
- grad_target: bfloat16 [4096, 2048], P('seq', 'head')
- grad_source: bfloat16 [4096, 2048], P('seq', 'head')
The draws below stay inside these ranges and needn't reach their ends.
Inputs may be any that keep to these rules, and one draw needn't show every extreme that they name: `target`: activations of order one, at most some rows much larger. band_start and band_end never fall from block to block; band_start[b] >= b - 1, band_start[b] < band_end[b] <= band_start[b] + 3, band_end[b] <= b + 3; some target block has a band of exactly 3 source blocks. `band_end`: see band_start.
All inputs are finite; a program needn't handle non-finite values.
Results may differ from the reference program's by a relative error of at most 0.02.
Values may be sent and summed in bfloat16 or wider, within the bound.
A program may use at most 64 MiB of HBM per device.

```python
import jax
import jax.numpy as jnp
from jax import lax

D = 2048
HEADS = 16
HEAD_DIM = 128
BLOCK = 64
MAXW = 3
TOK_DEV = 256
TOKENS = 4096
NBLK = 64
N_HEAD = 2


def band_pair(key):
    base = jax.random.fold_in(key, 7)
    first_key, second_key = jax.random.split(base)
    blocks = jnp.arange(NBLK, dtype=jnp.int32)
    lean = jax.random.randint(first_key, (NBLK,), 0, 2).astype(jnp.int32)
    lean = lean.at[NBLK - 1].set(1)
    shard_first = blocks % (TOK_DEV // BLOCK) == 0
    lean = jnp.where(shard_first, 0, lean).astype(jnp.int32)
    start = jnp.maximum(blocks - 1 + lean, 0)
    widths = jax.random.randint(second_key, (NBLK,), 1, MAXW + 1).astype(jnp.int32)
    widths = widths.at[0].set(1).at[NBLK // 2].set(MAXW)
    reach = lax.cummax(start + widths, axis=0)
    finish = jnp.minimum(jnp.minimum(reach, start + MAXW), NBLK)
    return (start.astype(jnp.int32), finish.astype(jnp.int32))


def draw_band_start(key, part):
    return band_pair(key)[0]


def draw_band_end(key, part):
    return band_pair(key)[1]


def draw_target(key, part):
    keys = jax.random.split(jax.random.fold_in(key, 11), 1)
    values = jax.random.truncated_normal(keys[0], -4.0, 4.0, (TOKENS, D), jnp.float32)
    return values.astype(jnp.bfloat16)


def steps_of(key, shape, shards, low, largest):
    loudness, own = 1.0, jax.random.fold_in(key, 6)
    for dim, shards_of in shards:
        heights = jnp.exp(jax.random.uniform(jax.random.fold_in(own, dim), (shards_of,), jnp.float32, low / len(shards), largest / len(shards)))
        loudness = loudness * jnp.repeat(heights, shape[dim] // shards_of).reshape([-1 if axis == dim else 1 for axis in range(len(shape))])
    return loudness


def bell_draw(stream_key, dims, scale, limit, cuts=(), kind=jnp.bfloat16):
    entries = scale * jax.random.normal(stream_key, dims, jnp.float32)
    if cuts:
        entries = entries * steps_of(stream_key, dims, cuts, -0.22, 0.18)
    return jnp.clip(entries, -limit, limit).astype(kind)


def setup_inputs(seed: int = 0) -> dict:
    seeds = jax.random.split(jax.random.key(seed), 10)
    return {
        "target": draw_target(jax.random.fold_in(seeds[9], 71), 0),
        "source": bell_draw(seeds[1], (TOKENS, D), 1.0, 6.0, ((0, 16), (1, 2))),
        "w_query": bell_draw(seeds[2], (D, D), D ** -0.5, 0.125, ((0, 16), (1, 2))),
        "w_key": bell_draw(seeds[3], (D, D), D ** -0.5, 0.125, ((0, 16), (1, 2))),
        "w_value": bell_draw(seeds[4], (D, D), D ** -0.5, 0.125, ((0, 16), (1, 2))),
        "w_out": bell_draw(seeds[5], (D, D), D ** -0.5, 0.125, ((0, 16), (1, 2))),
        "band_start": draw_band_start(jax.random.fold_in(seeds[9], 71), 0),
        "band_end": draw_band_end(jax.random.fold_in(seeds[9], 71), 0),
        "cotangent": bell_draw(seeds[8], (TOKENS, D), 1.0, 6.0, ((0, 16), (1, 2))),
    }


def group_sum(pairs):
    width = D // N_HEAD
    rows = pairs[0][0].shape[0]
    total = jnp.zeros((rows, D), jnp.float32)
    for group in range(N_HEAD):
        part = jnp.zeros((rows, D), jnp.float32)
        for left, right in pairs:
            part = part + lax.dot_general(left[:, group * width:(group + 1) * width], right[:, group * width:(group + 1) * width], (((1,), (1,)), ((), ())), preferred_element_type=jnp.float32)
        part = lax.optimization_barrier(part.astype(jnp.bfloat16))
        total = total + part.astype(jnp.float32)
    return total


def reference(target, source, w_query, w_key, w_value, w_out, band_start, band_end, cotangent):
    fone = jnp.float32
    half = jnp.bfloat16
    query = jnp.dot(target, w_query, preferred_element_type=fone).astype(half)
    key = jnp.dot(source, w_key, preferred_element_type=fone).astype(half)
    value = jnp.dot(source, w_value, preferred_element_type=fone).astype(half)
    span = MAXW * BLOCK
    first = jnp.clip(band_start * BLOCK, 0, TOKENS - span).astype(jnp.int32)
    rows_idx = first[:, None] + jnp.arange(span, dtype=jnp.int32)[None, :]
    key_block = rows_idx // BLOCK
    visible = (key_block >= band_start[:, None]) & (key_block < band_end[:, None])
    q_blocks = query.reshape(NBLK, BLOCK, HEADS, HEAD_DIM).astype(fone)
    k_blocks = key[rows_idx].reshape(NBLK, span, HEADS, HEAD_DIM).astype(fone)
    v_blocks = value[rows_idx].reshape(NBLK, span, HEADS, HEAD_DIM).astype(fone)
    scale = HEAD_DIM ** -0.5
    scores = jnp.einsum("nqhe,nkhe->nhqk", q_blocks, k_blocks) * scale
    scores = jnp.where(visible[:, None, None, :], scores, -jnp.inf)
    top = jnp.max(scores, axis=-1, keepdims=True)
    expo = jnp.exp(scores - top)
    prob = expo / jnp.sum(expo, axis=-1, keepdims=True)
    prob_b = lax.optimization_barrier(prob.astype(half)).astype(fone)
    context = jnp.einsum("nhqk,nkhe->nqhe", prob_b, v_blocks).astype(half)
    attended = group_sum([(context.reshape(TOKENS, D), w_out)]).astype(half)
    d_context = jnp.dot(cotangent, w_out, preferred_element_type=fone).astype(half)
    dc_blocks = d_context.reshape(NBLK, BLOCK, HEADS, HEAD_DIM).astype(fone)
    delta = jnp.sum(dc_blocks * context.astype(fone), axis=-1)
    delta = jnp.transpose(delta, (0, 2, 1))[..., None]
    d_prob = jnp.einsum("nqhe,nkhe->nhqk", dc_blocks, v_blocks)
    d_score = (prob * (d_prob - delta) * scale).astype(half)
    d_score = lax.optimization_barrier(d_score).astype(fone)
    d_query = jnp.einsum("nhqk,nkhe->nqhe", d_score, k_blocks).astype(half)
    dk_blocks = jnp.einsum("nhqk,nqhe->nkhe", d_score, q_blocks)
    dv_blocks = jnp.einsum("nhqk,nqhe->nkhe", prob_b, dc_blocks)
    flat = rows_idx.reshape(-1)
    d_key = jnp.zeros((TOKENS, D), fone).at[flat].add(dk_blocks.reshape(-1, D)).astype(half)
    d_value = jnp.zeros((TOKENS, D), fone).at[flat].add(dv_blocks.reshape(-1, D)).astype(half)
    grad_target = group_sum([(d_query.reshape(TOKENS, D), w_query)]).astype(half)
    grad_source = group_sum([(d_key, w_key), (d_value, w_value)]).astype(half)
    return (attended, grad_target, grad_source)
```

```python
import functools

import jax
import jax.numpy as jnp
from jax import lax
from jax.experimental import pallas as pl
from jax.experimental.pallas import tpu as pltpu
from jax.sharding import PartitionSpec as P

HEAD_DIM = 128
BLOCK = 64
MAXW = 3
CHIPS_Z = 4
CORES = 2
ACT_OF = (0, 0, 1, 2)
TILE = 256


def gather_kernel(
    seqs, heads, src_ref, tgt_ref, cot_ref, wk_ref, wv_ref, wq_ref, wo_ref,
    proj_ref, wall_ref, acts, z_send, y_send, c_send, w_recv, h_send, h_recv,
):
    chips_y = seqs // (CHIPS_Z * CORES)
    me = lax.axis_index("seq")
    hm = lax.axis_index("head")
    z = me // (chips_y * CORES)
    y = lax.rem(me // CORES, chips_y)
    c = lax.rem(me, CORES)
    own = (wk_ref, wv_ref, wq_ref, wo_ref)
    depth = wk_ref.shape[0]
    rows = src_ref.shape[0]
    feats = src_ref.shape[1]
    width = wk_ref.shape[1]
    has_up = z < CHIPS_Z - 1
    has_down = z > 0

    def seq_of(zz, yy, cc):
        return (zz * chips_y + yy) * CORES + cc

    def slot(w, s):
        return wall_ref.at[w, pl.ds(pl.multiple_of(s * depth, depth), depth)]

    def send(w, s, src, sem, to):
        return pltpu.make_async_remote_copy(
            src_ref=src, dst_ref=slot(w, s), send_sem=sem, recv_sem=w_recv.at[w, s],
            device_id={"seq": to}, device_id_type=pl.DeviceIdType.MESH,
        )

    def arrived(w, s):
        send(w, s, slot(w, s), z_send.at[w, 0, 0], me).wait_recv()

    def up(w, zz, src):
        return send(w, seq_of(zz, y, c), src, z_send.at[w, zz, 0], me + chips_y * CORES)

    def down(w, zz, src):
        return send(w, seq_of(zz, y, c), src, z_send.at[w, zz, 1], me - chips_y * CORES)

    def across(w, zz, off, src):
        return send(
            w, seq_of(zz, y, c), src, y_send.at[w, zz, off],
            seq_of(z, lax.rem(y + off, chips_y), c),
        )

    def beside(w, zz, yy, src):
        return send(w, seq_of(zz, yy, c), src, c_send.at[w, zz, yy], seq_of(z, y, 1 - c))

    barrier = pltpu.get_barrier_semaphore()

    def greet(axis, to):
        pl.semaphore_signal(
            barrier, inc=1, device_id={axis: to}, device_id_type=pl.DeviceIdType.MESH
        )

    @pl.when(has_up)
    def _():
        greet("seq", me + chips_y * CORES)

    @pl.when(has_down)
    def _():
        greet("seq", me - chips_y * CORES)

    for off in range(1, chips_y):
        greet("seq", seq_of(z, lax.rem(y + off, chips_y), c))
    greet("seq", seq_of(z, y, 1 - c))
    for off in range(1, heads):
        greet("head", lax.rem(hm + off, heads))
    pl.semaphore_wait(
        barrier,
        has_up.astype(jnp.int32) + has_down.astype(jnp.int32) + chips_y - 1 + 1 + heads - 1,
    )

    def act_copy(a, off):
        ref = (src_ref, tgt_ref, cot_ref)[a]
        return pltpu.make_async_remote_copy(
            src_ref=ref, dst_ref=acts.at[a, hm], send_sem=h_send.at[a, off],
            recv_sem=h_recv.at[a, hm], device_id={"head": lax.rem(hm + off, heads)},
            device_id_type=pl.DeviceIdType.MESH,
        )

    def act_arrived(a, off):
        came = lax.rem(hm + off, heads)
        pltpu.make_async_remote_copy(
            src_ref=acts.at[a, came], dst_ref=acts.at[a, came], send_sem=h_send.at[a, off],
            recv_sem=h_recv.at[a, came], device_id={"head": came},
            device_id_type=pl.DeviceIdType.MESH,
        ).wait_recv()

    def start_own(w):
        ref = own[w]

        @pl.when(has_up)
        def _():
            up(w, z, ref).start()

        @pl.when(has_down)
        def _():
            down(w, z, ref).start()

        for off in range(1, chips_y):
            across(w, z, off, ref).start()
        beside(w, z, y, ref).start()

    def relay_z(w, d):
        low, high = z - d, z + d

        @pl.when(low >= 0)
        def _():
            s = seq_of(low, y, c)
            arrived(w, s)

            @pl.when(has_up)
            def _():
                up(w, low, slot(w, s)).start()

            for off in range(1, chips_y):
                across(w, low, off, slot(w, s)).start()
            beside(w, low, y, slot(w, s)).start()

        @pl.when(high < CHIPS_Z)
        def _():
            s = seq_of(high, y, c)
            arrived(w, s)

            @pl.when(has_down)
            def _():
                down(w, high, slot(w, s)).start()

            for off in range(1, chips_y):
                across(w, high, off, slot(w, s)).start()
            beside(w, high, y, slot(w, s)).start()

    def relay_y(w, d):
        def one(zz):
            for off in range(1, chips_y):
                yy = lax.rem(y + off, chips_y)
                s = seq_of(zz, yy, c)
                arrived(w, s)
                beside(w, zz, yy, slot(w, s)).start()

        @pl.when(z - d >= 0)
        def _():
            one(z - d)

        if d > 0:

            @pl.when(z + d < CHIPS_Z)
            def _():
                one(z + d)

    def gather(w):
        relay_z(w, 1)
        relay_y(w, 0)
        relay_z(w, 2)
        relay_y(w, 1)
        relay_z(w, 3)
        relay_y(w, 2)
        relay_y(w, 3)

    def others(w):
        def one(i, carry):
            arrived(w, i * CORES + 1 - c)
            return carry

        lax.fori_loop(0, seqs // CORES, one, 0)

    def project(w):
        tile = min(TILE, width)

        def columns(j, carry):
            cols = pl.ds(pl.multiple_of(j * tile, tile), tile)

            def part(h, total):
                return total + jnp.dot(
                    acts[ACT_OF[w], h],
                    wall_ref[w, pl.ds(pl.multiple_of(h * feats, feats), feats), cols],
                    preferred_element_type=jnp.float32,
                )

            total = lax.fori_loop(0, heads, part, jnp.zeros((rows, tile), jnp.float32))
            proj_ref[w, :, cols] = total.astype(proj_ref.dtype)
            return carry

        lax.fori_loop(0, width // tile, columns, 0)

    start_own(0)
    for off in range(1, heads):
        act_copy(0, off).start()
    start_own(1)
    for a in (1, 2):
        for off in range(1, heads):
            act_copy(a, off).start()
    for w in range(4):
        wall_ref[w, pl.ds(pl.multiple_of(me * depth, depth), depth)] = own[w][...]
    for a, ref in enumerate((src_ref, tgt_ref, cot_ref)):
        acts[a, hm] = ref[...]
    seen = set()
    for w in range(4):
        gather(w)
        if w + 2 < 4:
            start_own(w + 2)
        others(w)
        if ACT_OF[w] not in seen:
            seen.add(ACT_OF[w])
            for off in range(1, heads):
                act_arrived(ACT_OF[w], off)
        project(w)

    def drain(w):
        for zz in range(CHIPS_Z):

            @pl.when(has_up & (zz <= z))
            def _():
                up(w, zz, own[0]).wait_send()

            @pl.when(has_down & (zz >= z))
            def _():
                down(w, zz, own[0]).wait_send()

            for off in range(1, chips_y):
                across(w, zz, off, own[0]).wait_send()

            def side(yy, carry):
                beside(w, zz, yy, own[0]).wait_send()
                return carry

            lax.fori_loop(0, chips_y, side, 0)

    for w in range(4):
        drain(w)
    for a in range(3):
        for off in range(1, heads):
            act_copy(a, off).wait_send()


def gather_and_project(seqs, heads, target, source, cotangent, wk, wv, wq, wo):
    rows, feats = target.shape
    depth, width = wk.shape
    chips_y = seqs // (CHIPS_Z * CORES)
    vmem = pl.BlockSpec(memory_space=pltpu.VMEM)
    return pl.pallas_call(
        functools.partial(gather_kernel, seqs, heads),
        out_shape=(
            jax.ShapeDtypeStruct((4, rows, width), jnp.bfloat16),
            jax.ShapeDtypeStruct((4, seqs * depth, width), jnp.bfloat16),
        ),
        in_specs=[vmem] * 7,
        out_specs=(vmem, vmem),
        scratch_shapes=[
            pltpu.VMEM((3, heads, rows, feats), jnp.bfloat16),
            pltpu.SemaphoreType.DMA((4, CHIPS_Z, 2)),
            pltpu.SemaphoreType.DMA((4, CHIPS_Z, chips_y)),
            pltpu.SemaphoreType.DMA((4, CHIPS_Z, chips_y)),
            pltpu.SemaphoreType.DMA((4, seqs)),
            pltpu.SemaphoreType.DMA((3, heads)),
            pltpu.SemaphoreType.DMA((3, heads)),
        ],
        compiler_params=pltpu.CompilerParams(
            collective_id=0, has_side_effects=True, vmem_limit_bytes=48 * 1024 * 1024
        ),
        cost_estimate=pl.CostEstimate(
            flops=8 * rows * seqs * depth * width,
            bytes_accessed=8 * seqs * depth * width,
            transcendentals=0,
        ),
    )(source, target, cotangent, wk, wv, wq, wo)


def passed_along(shard, axis, by):
    count = lax.axis_size(axis)
    pairs = [(i, i + by) for i in range(count) if 0 <= i + by < count]
    return lax.ppermute(shard, axis, pairs)


def times_transpose(left, right):
    return lax.dot_general(
        left, right, (((1,), (1,)), ((), ())), preferred_element_type=jnp.float32
    )


def summed_over_heads(term):
    count = lax.axis_size("head")
    term = term.astype(jnp.bfloat16)
    if count != 2:
        return lax.psum_scatter(term, "head", scatter_dimension=1, tiled=True)
    feats = term.shape[1] // 2
    hm = lax.axis_index("head")
    away = lax.dynamic_slice_in_dim(term, (1 - hm) * feats, feats, 1)
    kept = lax.dynamic_slice_in_dim(term, hm * feats, feats, 1)
    came = lax.ppermute(away, "head", [(0, 1), (1, 0)])
    return (kept.astype(jnp.float32) + came.astype(jnp.float32)).astype(jnp.bfloat16)


def per_device(target, source, w_query, w_key, w_value, w_out, band_start, band_end, cotangent):
    fone = jnp.float32
    half = jnp.bfloat16
    rows = target.shape[0]
    width = w_query.shape[1]
    heads = width // HEAD_DIM
    blocks = rows // BLOCK
    right_rows = (MAXW - 1) * BLOCK
    scale = HEAD_DIM ** (-0.5)
    proj, wall = gather_and_project(
        lax.axis_size("seq"), lax.axis_size("head"),
        target, source, cotangent, w_key, w_value, w_query, w_out,
    )
    wk, wv, wq, wo = wall[0], wall[1], wall[2], wall[3]
    query, d_context = proj[2], proj[3]
    packed = jnp.concatenate([proj[0], proj[1]], 1)
    from_prev = passed_along(packed[rows - BLOCK :], "seq", 1)
    from_next = passed_along(packed[:right_rows], "seq", -1)
    window = jnp.concatenate([from_prev, packed, from_next], 0)
    span = window.shape[0]
    anchor = lax.axis_index("seq") * blocks - 1
    low_rows = jnp.repeat(band_start - anchor, BLOCK)[:, None]
    high_rows = jnp.repeat(band_end - anchor, BLOCK)[:, None]
    key_block = (jnp.arange(span, dtype=jnp.int32) // BLOCK)[None, :]
    visible = (key_block >= low_rows) & (key_block < high_rows)
    q = query.reshape(rows, heads, HEAD_DIM)
    dc = d_context.reshape(rows, heads, HEAD_DIM)
    kv = window.reshape(span, 2 * heads, HEAD_DIM)
    k, v = kv[:, :heads], kv[:, heads:]
    scores = jnp.einsum("qhe,khe->hqk", q, k, preferred_element_type=fone) * scale
    scores = jnp.where(visible[None], scores, -jnp.inf)
    top = jnp.max(scores, axis=-1, keepdims=True)
    expo = jnp.exp(scores - top)
    prob = expo / jnp.sum(expo, axis=-1, keepdims=True)
    prob_b = prob.astype(half)
    context = jnp.einsum("hqk,khe->qhe", prob_b, v, preferred_element_type=fone).astype(half)
    attended = summed_over_heads(times_transpose(context.reshape(rows, width), wo))
    delta = jnp.sum(dc.astype(fone) * context.astype(fone), axis=-1)
    delta = jnp.transpose(delta, (1, 0))[..., None]
    d_prob = jnp.einsum("qhe,khe->hqk", dc, v, preferred_element_type=fone)
    d_score = (prob * (d_prob - delta) * scale).astype(half)
    d_query = jnp.einsum("hqk,khe->qhe", d_score, k, preferred_element_type=fone).astype(half)
    dk = jnp.einsum("hqk,qhe->khe", d_score, q, preferred_element_type=fone)
    dv = jnp.einsum("hqk,qhe->khe", prob_b, dc, preferred_element_type=fone)
    d_window = jnp.concatenate([dk.reshape(span, width), dv.reshape(span, width)], 1)
    back_next = passed_along(d_window[:BLOCK], "seq", -1)
    back_prev = passed_along(d_window[BLOCK + rows :], "seq", 1)
    grad_target = summed_over_heads(times_transpose(d_query.reshape(rows, width), wq))
    owned = d_window[BLOCK : BLOCK + rows]
    owned = owned.at[rows - BLOCK :].add(back_next)
    owned = owned.at[:right_rows].add(back_prev)
    d_key = owned[:, :width].astype(half)
    d_value = owned[:, width:].astype(half)
    grad_source = summed_over_heads(times_transpose(d_key, wk) + times_transpose(d_value, wv))
    return (attended, grad_target, grad_source)


def solution(mesh):
    both = P("seq", "head")
    return jax.shard_map(
        per_device,
        mesh=mesh,
        in_specs=(both,) * 6 + (P("seq"), P("seq"), both),
        out_specs=(both,) * 3,
        check_vma=False,
    )
```

```python
import functools

import jax
import jax.numpy as jnp
from jax import lax
from jax.experimental import pallas as pl
from jax.experimental.pallas import tpu as pltpu
from jax.sharding import PartitionSpec as P

HEAD_DIM = 128
BLOCK = 64
MAXW = 3
CHIPS_Z = 4
CORES = 2
ACT_OF = (0, 0, 1, 2)
TILE = 256


def sublayer_kernel(
    seqs, heads, src_ref, tgt_ref, cot_ref, wk_ref, wv_ref, wq_ref, wo_ref, bias_ref,
    att_ref, gt_ref, gs_ref,
    wall_ref, acts, kvw, qd, prob_ref, probb_ref, ctx, dq, dkv, dkvb,
    edge_out_low, edge_out_high, edge_in_low, edge_in_high, outbox, inbox,
    z_send, y_send, c_send, w_recv, h_send, h_recv, own_sem,
    f_send, f_recv, b_send, b_recv, o_send, o_recv,
):
    chips_y = seqs // (CHIPS_Z * CORES)
    me = lax.axis_index("seq")
    hm = lax.axis_index("head")
    z = me // (chips_y * CORES)
    y = lax.rem(me // CORES, chips_y)
    c = lax.rem(me, CORES)
    own = (wk_ref, wv_ref, wq_ref, wo_ref)
    depth = wk_ref.shape[0]
    rows = src_ref.shape[0]
    feats = src_ref.shape[1]
    width = wk_ref.shape[1]
    has_up = z < CHIPS_Z - 1
    has_down = z > 0
    has_next = me < seqs - 1
    has_prev = me > 0
    span = kvw.shape[1]
    right = (MAXW - 1) * BLOCK
    local_heads = width // HEAD_DIM
    scale = HEAD_DIM ** (-0.5)
    layer = seqs * depth // CHIPS_Z
    piece_cols = outbox.shape[3]
    pieces = outbox.shape[1]
    subs = feats // piece_cols
    per_layer = layer // piece_cols
    outs = (att_ref, gt_ref, gs_ref)
    far = me + 2 * c - 1
    has_far = (far >= 0) & (far < seqs)

    def seq_of(zz, yy, cc):
        return (zz * chips_y + yy) * CORES + cc

    def slot(w, s):
        return wall_ref.at[w, pl.ds(pl.multiple_of(s * depth, depth), depth)]

    def send(w, s, src, sem, to):
        return pltpu.make_async_remote_copy(
            src_ref=src, dst_ref=slot(w, s), send_sem=sem, recv_sem=w_recv.at[w, s],
            device_id={"seq": to}, device_id_type=pl.DeviceIdType.MESH,
        )

    def arrived(w, s):
        send(w, s, slot(w, s), z_send.at[w, 0, 0], me).wait_recv()

    def up(w, zz, src):
        return send(w, seq_of(zz, y, c), src, z_send.at[w, zz, 0], me + chips_y * CORES)

    def down(w, zz, src):
        return send(w, seq_of(zz, y, c), src, z_send.at[w, zz, 1], me - chips_y * CORES)

    def across(w, zz, off, src):
        return send(
            w, seq_of(zz, y, c), src, y_send.at[w, zz, off],
            seq_of(z, lax.rem(y + off, chips_y), c),
        )

    def beside(w, zz, yy, src):
        return send(w, seq_of(zz, yy, c), src, c_send.at[w, zz, yy], seq_of(z, y, 1 - c))

    barrier = pltpu.get_barrier_semaphore()

    def greet(axis, to):
        pl.semaphore_signal(
            barrier, inc=1, device_id={axis: to}, device_id_type=pl.DeviceIdType.MESH
        )

    @pl.when(has_up)
    def _():
        greet("seq", me + chips_y * CORES)

    @pl.when(has_down)
    def _():
        greet("seq", me - chips_y * CORES)

    for off in range(1, chips_y):
        greet("seq", seq_of(z, lax.rem(y + off, chips_y), c))
    greet("seq", seq_of(z, y, 1 - c))

    @pl.when(has_far)
    def _():
        greet("seq", far)

    for off in range(1, heads):
        greet("head", lax.rem(hm + off, heads))
    pl.semaphore_wait(
        barrier,
        has_up.astype(jnp.int32)
        + has_down.astype(jnp.int32)
        + has_far.astype(jnp.int32)
        + (chips_y - 1 + 1 + heads - 1),
    )

    def act_copy(a, off):
        ref = (src_ref, tgt_ref, cot_ref)[a]
        return pltpu.make_async_remote_copy(
            src_ref=ref, dst_ref=acts.at[a, hm], send_sem=h_send.at[a, off],
            recv_sem=h_recv.at[a, hm], device_id={"head": lax.rem(hm + off, heads)},
            device_id_type=pl.DeviceIdType.MESH,
        )

    def act_arrived(a, off):
        came = lax.rem(hm + off, heads)
        pltpu.make_async_remote_copy(
            src_ref=acts.at[a, came], dst_ref=acts.at[a, came], send_sem=h_send.at[a, off],
            recv_sem=h_recv.at[a, came], device_id={"head": came},
            device_id_type=pl.DeviceIdType.MESH,
        ).wait_recv()

    def start_own(w):
        ref = own[w]

        @pl.when(has_up)
        def _():
            up(w, z, ref).start()

        @pl.when(has_down)
        def _():
            down(w, z, ref).start()

        for off in range(1, chips_y):
            across(w, z, off, ref).start()
        beside(w, z, y, ref).start()

    def relay_z(w, d):
        low, high = z - d, z + d

        @pl.when(low >= 0)
        def _():
            s = seq_of(low, y, c)
            arrived(w, s)

            @pl.when(has_up)
            def _():
                up(w, low, slot(w, s)).start()

            for off in range(1, chips_y):
                across(w, low, off, slot(w, s)).start()
            beside(w, low, y, slot(w, s)).start()

        @pl.when(high < CHIPS_Z)
        def _():
            s = seq_of(high, y, c)
            arrived(w, s)

            @pl.when(has_down)
            def _():
                down(w, high, slot(w, s)).start()

            for off in range(1, chips_y):
                across(w, high, off, slot(w, s)).start()
            beside(w, high, y, slot(w, s)).start()

    def relay_y(w, d):
        def one(zz):
            for off in range(1, chips_y):
                yy = lax.rem(y + off, chips_y)
                s = seq_of(zz, yy, c)
                arrived(w, s)
                beside(w, zz, yy, slot(w, s)).start()

        @pl.when(z - d >= 0)
        def _():
            one(z - d)

        if d > 0:

            @pl.when(z + d < CHIPS_Z)
            def _():
                one(z + d)

    def others(w):
        def one(i, carry):
            arrived(w, i * CORES + 1 - c)
            return carry

        lax.fori_loop(0, seqs // CORES, one, 0)

    def others_of_layer(w, zz):
        def one(yy, carry):
            arrived(w, seq_of(zz, yy, 1 - c))
            return carry

        lax.fori_loop(0, chips_y, one, 0)

    def project(w):
        tile = min(TILE, width)

        def columns(j, carry):
            cols = pl.ds(pl.multiple_of(j * tile, tile), tile)

            def part(h, total):
                return total + jnp.dot(
                    acts[ACT_OF[w], h],
                    wall_ref[w, pl.ds(pl.multiple_of(h * feats, feats), feats), cols],
                    preferred_element_type=jnp.float32,
                )

            total = lax.fori_loop(0, heads, part, jnp.zeros((rows, tile), jnp.float32))
            if w < 2:
                kvw[w, BLOCK : BLOCK + rows, cols] = total.astype(jnp.bfloat16)
            else:
                qd[w - 2, :, cols] = total.astype(jnp.bfloat16)
            return carry

        lax.fori_loop(0, width // tile, columns, 0)

    def halo_next(w):
        return pltpu.make_async_remote_copy(
            src_ref=kvw.at[w, pl.ds(rows, BLOCK)], dst_ref=kvw.at[w, pl.ds(0, BLOCK)],
            send_sem=f_send.at[w, 0], recv_sem=f_recv.at[w, 0],
            device_id={"seq": me + 1}, device_id_type=pl.DeviceIdType.MESH,
        )

    def halo_prev(w):
        return pltpu.make_async_remote_copy(
            src_ref=kvw.at[w, pl.ds(BLOCK, right)], dst_ref=kvw.at[w, pl.ds(BLOCK + rows, right)],
            send_sem=f_send.at[w, 1], recv_sem=f_recv.at[w, 1],
            device_id={"seq": me - 1}, device_id_type=pl.DeviceIdType.MESH,
        )

    def edge_next():
        return pltpu.make_async_remote_copy(
            src_ref=edge_out_high, dst_ref=edge_in_low, send_sem=b_send.at[0],
            recv_sem=b_recv.at[0], device_id={"seq": me + 1},
            device_id_type=pl.DeviceIdType.MESH,
        )

    def edge_prev():
        return pltpu.make_async_remote_copy(
            src_ref=edge_out_low, dst_ref=edge_in_high, send_sem=b_send.at[1],
            recv_sem=b_recv.at[1], device_id={"seq": me - 1},
            device_id_type=pl.DeviceIdType.MESH,
        )

    def halo_start(w):
        @pl.when(has_next)
        def _():
            halo_next(w).start()

        @pl.when(has_prev)
        def _():
            halo_prev(w).start()

    def halo_arrived():
        for w in range(2):

            @pl.when(has_prev)
            def _():
                halo_next(w).wait_recv()

            @pl.when(has_next)
            def _():
                halo_prev(w).wait_recv()

    def head_columns(h):
        return pl.ds(pl.multiple_of(h * HEAD_DIM, HEAD_DIM), HEAD_DIM)

    def dot_t(left, right_):
        return lax.dot_general(
            left, right_, (((1,), (1,)), ((), ())), preferred_element_type=jnp.float32
        )

    def dot_over_rows(left, right_):
        return lax.dot_general(
            left, right_, (((0,), (0,)), ((), ())), preferred_element_type=jnp.float32
        )

    def forward(h, carry):
        cols = head_columns(h)
        scores = dot_t(qd[0, :, cols], kvw[0, :, cols]) * scale + bias_ref[...]
        expo = jnp.exp(scores - jnp.max(scores, axis=1, keepdims=True))
        prob = expo * (1.0 / jnp.sum(expo, axis=1, keepdims=True))
        rounded = prob.astype(jnp.bfloat16)
        prob_ref[h] = prob
        probb_ref[h] = rounded
        ctx[:, cols] = jnp.dot(
            rounded, kvw[1, :, cols], preferred_element_type=jnp.float32
        ).astype(jnp.bfloat16)
        return carry

    def backward(h, carry):
        cols = head_columns(h)
        d_ctx = qd[1, :, cols]
        delta = jnp.sum(
            d_ctx.astype(jnp.float32) * ctx[:, cols].astype(jnp.float32), axis=1, keepdims=True
        )
        d_prob = dot_t(d_ctx, kvw[1, :, cols])
        d_score = (prob_ref[h] * (d_prob - delta) * scale).astype(jnp.bfloat16)
        dq[:, cols] = jnp.dot(
            d_score, kvw[0, :, cols], preferred_element_type=jnp.float32
        ).astype(jnp.bfloat16)
        dkv[0, :, cols] = dot_over_rows(d_score, qd[0, :, cols])
        dkv[1, :, cols] = dot_over_rows(probb_ref[h], d_ctx)
        return carry

    def out_copy(o, piece):
        to = piece // subs
        return pltpu.make_async_remote_copy(
            src_ref=outbox.at[o, piece], dst_ref=inbox.at[o, hm, lax.rem(piece, subs)],
            send_sem=o_send.at[o, piece], recv_sem=o_recv.at[o, hm, lax.rem(piece, subs)],
            device_id={"head": to}, device_id_type=pl.DeviceIdType.MESH,
        )

    def put_piece(o, piece):
        feat_rows = pl.ds(pl.multiple_of(piece * piece_cols, piece_cols), piece_cols)
        if o == 0:
            term = dot_t(ctx[...], wall_ref[3, feat_rows])
        elif o == 1:
            term = dot_t(dq[...], wall_ref[2, feat_rows])
        else:
            term = dot_t(dkvb[0], wall_ref[0, feat_rows]) + dot_t(dkvb[1], wall_ref[1, feat_rows])
        outbox[o, piece] = term.astype(jnp.bfloat16)

        @pl.when(piece // subs != hm)
        def _():
            out_copy(o, piece).start()

    def put_all(o):
        def one(i, carry):
            put_piece(o, lax.rem((hm + 1) * subs + i, pieces))
            return carry

        lax.fori_loop(0, pieces, one, 0)

    def finish(o):
        for sub in range(subs):
            total = outbox[o, hm * subs + sub].astype(jnp.float32)
            for off in range(1, heads):
                came = lax.rem(hm + off, heads)
                pltpu.make_async_remote_copy(
                    src_ref=inbox.at[o, came, sub], dst_ref=inbox.at[o, came, sub],
                    send_sem=o_send.at[o, 0], recv_sem=o_recv.at[o, came, sub],
                    device_id={"head": came}, device_id_type=pl.DeviceIdType.MESH,
                ).wait_recv()
                total = total + inbox[o, came, sub].astype(jnp.float32)
            outs[o][:, sub * piece_cols : (sub + 1) * piece_cols] = total.astype(jnp.bfloat16)

    def own_copy(w):
        return pltpu.make_async_copy(own[w], slot(w, me), own_sem.at[w])

    def own_act(a):
        ref = (src_ref, tgt_ref, cot_ref)[a]
        return pltpu.make_async_copy(ref, acts.at[a, hm], own_sem.at[4 + a])

    start_own(0)
    for off in range(1, heads):
        act_copy(0, off).start()
    start_own(1)
    for a in (1, 2):
        for off in range(1, heads):
            act_copy(a, off).start()
    for w in range(4):
        own_copy(w).start()
    for a in range(3):
        own_act(a).start()
    kvw[:, BLOCK + rows + right :] = jnp.zeros_like(kvw[:, BLOCK + rows + right :])

    @pl.when(me == 0)
    def _():
        kvw[:, :BLOCK] = jnp.zeros_like(kvw[:, :BLOCK])
        edge_in_low[...] = jnp.zeros_like(edge_in_low)

    @pl.when(me == seqs - 1)
    def _():
        kvw[:, BLOCK + rows : BLOCK + rows + right] = jnp.zeros_like(
            kvw[:, BLOCK + rows : BLOCK + rows + right]
        )
        edge_in_high[...] = jnp.zeros_like(edge_in_high)

    def acts_ready(a):
        own_act(a).wait()
        for off in range(1, heads):
            act_arrived(a, off)

    def complete(w, first):
        if first:
            acts_ready(ACT_OF[w])
        own_copy(w).wait()
        others(w)
        project(w)

    def attended_layer(zz):
        others_of_layer(3, zz)

        def one(j, carry):
            put_piece(0, zz * per_layer + j)
            return carry

        lax.fori_loop(0, per_layer, one, 0)

    def attended_at(d):
        @pl.when(z - d >= 0)
        def _():
            attended_layer(z - d)

        if d > 0:

            @pl.when(z + d < CHIPS_Z)
            def _():
                attended_layer(z + d)

    def gather(w, work):
        steps = [
            lambda: relay_z(w, 1), lambda: relay_y(w, 0), lambda: relay_z(w, 2),
            lambda: relay_y(w, 1), lambda: relay_z(w, 3), lambda: relay_y(w, 2),
            lambda: relay_y(w, 3),
        ]
        for i, step in enumerate(steps):
            step()
            for unit in work.get(i, ()):
                unit()

    half = local_heads // 2
    gather(0, {})
    start_own(2)
    gather(1, {0: [lambda: complete(0, True), lambda: halo_start(0)]})
    start_own(3)
    gather(2, {0: [lambda: complete(1, False), lambda: halo_start(1)]})
    gather(
        3,
        {
            0: [lambda: complete(2, True)],
            1: [halo_arrived, lambda: lax.fori_loop(0, half, forward, 0)],
            2: [lambda: lax.fori_loop(half, local_heads, forward, 0)],
            3: [lambda: own_copy(3).wait(), lambda: attended_at(0)],
            4: [lambda: attended_at(1)],
            5: [lambda: attended_at(2)],
            6: [lambda: attended_at(3)],
        },
    )
    acts_ready(2)
    project(3)
    lax.fori_loop(0, local_heads, backward, 0)
    edge_out_low[...] = dkv[:, :BLOCK].astype(jnp.bfloat16)
    edge_out_high[...] = dkv[:, BLOCK + rows : BLOCK + rows + right].astype(jnp.bfloat16)

    @pl.when(has_next)
    def _():
        edge_next().start()

    @pl.when(has_prev)
    def _():
        edge_prev().start()

    put_all(1)

    @pl.when(has_prev)
    def _():
        edge_next().wait_recv()

    @pl.when(has_next)
    def _():
        edge_prev().wait_recv()

    middle = rows - BLOCK
    dkvb[:, :right] = (
        dkv[:, BLOCK : BLOCK + right] + edge_in_low[...].astype(jnp.float32)
    ).astype(jnp.bfloat16)
    if middle > right:
        dkvb[:, right:middle] = dkv[:, BLOCK + right : BLOCK + middle].astype(jnp.bfloat16)
    dkvb[:, middle:] = (
        dkv[:, BLOCK + middle : BLOCK + rows] + edge_in_high[...].astype(jnp.float32)
    ).astype(jnp.bfloat16)
    put_all(2)
    for o in range(3):
        finish(o)

    def drain(w):
        for zz in range(CHIPS_Z):

            @pl.when(has_up & (zz <= z))
            def _():
                up(w, zz, own[0]).wait_send()

            @pl.when(has_down & (zz >= z))
            def _():
                down(w, zz, own[0]).wait_send()

            for off in range(1, chips_y):
                across(w, zz, off, own[0]).wait_send()

            def side(yy, carry):
                beside(w, zz, yy, own[0]).wait_send()
                return carry

            lax.fori_loop(0, chips_y, side, 0)

    for w in range(4):
        drain(w)
    for a in range(3):
        for off in range(1, heads):
            act_copy(a, off).wait_send()

    def out_drain(o, piece):
        @pl.when(piece // subs != hm)
        def _():
            out_copy(o, piece).wait_send()

    for o in range(3):
        for piece in range(pieces):
            out_drain(o, piece)

    @pl.when(has_next)
    def _():
        edge_next().wait_send()
        for w in range(2):
            halo_next(w).wait_send()

    @pl.when(has_prev)
    def _():
        edge_prev().wait_send()
        for w in range(2):
            halo_prev(w).wait_send()


def sublayer(seqs, heads, target, source, cotangent, wk, wv, wq, wo, bias):
    rows, feats = target.shape
    depth, width = wk.shape
    span = bias.shape[1]
    local_heads = width // HEAD_DIM
    right = (MAXW - 1) * BLOCK
    chips_y = seqs // (CHIPS_Z * CORES)
    piece_cols = min(feats, seqs * depth // CHIPS_Z)
    pieces = seqs * depth // piece_cols
    subs = feats // piece_cols
    vmem = pl.BlockSpec(memory_space=pltpu.VMEM)
    hbm = pl.BlockSpec(memory_space=pl.ANY)
    half, fone = jnp.bfloat16, jnp.float32
    return pl.pallas_call(
        functools.partial(sublayer_kernel, seqs, heads),
        out_shape=(jax.ShapeDtypeStruct((rows, feats), half),) * 3,
        in_specs=[hbm] * 7 + [vmem],
        out_specs=(vmem,) * 3,
        scratch_shapes=[
            pltpu.VMEM((4, seqs * depth, width), half),
            pltpu.VMEM((3, heads, rows, feats), half),
            pltpu.VMEM((2, span, width), half),
            pltpu.VMEM((2, rows, width), half),
            pltpu.VMEM((local_heads, rows, span), fone),
            pltpu.VMEM((local_heads, rows, span), half),
            pltpu.VMEM((rows, width), half),
            pltpu.VMEM((rows, width), half),
            pltpu.VMEM((2, span, width), fone),
            pltpu.VMEM((2, rows, width), half),
            pltpu.VMEM((2, BLOCK, width), half),
            pltpu.VMEM((2, right, width), half),
            pltpu.VMEM((2, right, width), half),
            pltpu.VMEM((2, BLOCK, width), half),
            pltpu.VMEM((3, pieces, rows, piece_cols), half),
            pltpu.VMEM((3, heads, subs, rows, piece_cols), half),
            pltpu.SemaphoreType.DMA((4, CHIPS_Z, 2)),
            pltpu.SemaphoreType.DMA((4, CHIPS_Z, chips_y)),
            pltpu.SemaphoreType.DMA((4, CHIPS_Z, chips_y)),
            pltpu.SemaphoreType.DMA((4, seqs)),
            pltpu.SemaphoreType.DMA((3, heads)),
            pltpu.SemaphoreType.DMA((3, heads)),
            pltpu.SemaphoreType.DMA((7,)),
            pltpu.SemaphoreType.DMA((2, 2)),
            pltpu.SemaphoreType.DMA((2, 2)),
            pltpu.SemaphoreType.DMA((2,)),
            pltpu.SemaphoreType.DMA((2,)),
            pltpu.SemaphoreType.DMA((3, pieces)),
            pltpu.SemaphoreType.DMA((3, heads, subs)),
        ],
        compiler_params=pltpu.CompilerParams(
            collective_id=0, has_side_effects=True, vmem_limit_bytes=56 * 1024 * 1024
        ),
        cost_estimate=pl.CostEstimate(
            flops=16 * rows * seqs * depth * width,
            bytes_accessed=8 * seqs * depth * width,
            transcendentals=local_heads * rows * span,
        ),
    )(source, target, cotangent, wk, wv, wq, wo, bias)


def per_device(target, source, w_query, w_key, w_value, w_out, band_start, band_end, cotangent):
    rows = target.shape[0]
    blocks = rows // BLOCK
    span = -(-(rows + MAXW * BLOCK) // 128) * 128
    anchor = lax.axis_index("seq") * blocks - 1
    low_rows = jnp.repeat(band_start - anchor, BLOCK)[:, None]
    high_rows = jnp.repeat(band_end - anchor, BLOCK)[:, None]
    key_block = (jnp.arange(span, dtype=jnp.int32) // BLOCK)[None, :]
    visible = (key_block >= low_rows) & (key_block < high_rows)
    bias = jnp.where(visible, 0.0, -jnp.inf).astype(jnp.float32)
    return sublayer(
        lax.axis_size("seq"), lax.axis_size("head"),
        target, source, cotangent, w_key, w_value, w_query, w_out, bias,
    )


def solution(mesh):
    both = P("seq", "head")
    return jax.shard_map(
        per_device,
        mesh=mesh,
        in_specs=(both,) * 6 + (P("seq"), P("seq"), both),
        out_specs=(both,) * 3,
        check_vma=False,
    )
```

```python
import functools

import jax
import jax.numpy as jnp
from jax import lax
from jax.experimental import pallas as pl
from jax.experimental.pallas import tpu as pltpu
from jax.sharding import PartitionSpec as P

HEAD_DIM = 128
BLOCK = 64
MAXW = 3
CHIPS_Z = 4
CORES = 2
ACT_OF = (0, 0, 1, 2)
TILE = 256


def sublayer_kernel(
    seqs, heads, src_ref, tgt_ref, cot_ref, wk_ref, wv_ref, wq_ref, wo_ref, bias_ref,
    att_ref, gt_ref, gs_ref,
    wall_ref, acts, kvw, qd, prob_ref, probb_ref, dscore_ref, ctx, dq, dkv, dkvb,
    edge_out_low, edge_out_high, edge_in_low, edge_in_high, outbox, inbox,
    z_send, y_send, c_send, w_recv, h_send, h_recv, own_sem,
    f_send, f_recv, b_send, b_recv, o_send, o_recv,
):
    chips_y = seqs // (CHIPS_Z * CORES)
    me = lax.axis_index("seq")
    hm = lax.axis_index("head")
    z = me // (chips_y * CORES)
    y = lax.rem(me // CORES, chips_y)
    c = lax.rem(me, CORES)
    own = (wk_ref, wv_ref, wq_ref, wo_ref)
    depth = wk_ref.shape[0]
    rows = src_ref.shape[0]
    feats = src_ref.shape[1]
    width = wk_ref.shape[1]
    has_up = z < CHIPS_Z - 1
    has_down = z > 0
    has_next = me < seqs - 1
    has_prev = me > 0
    span = kvw.shape[1]
    right = (MAXW - 1) * BLOCK
    local_heads = width // HEAD_DIM
    scale = HEAD_DIM ** (-0.5)
    layer = seqs * depth // CHIPS_Z
    piece_cols = outbox.shape[3]
    pieces = outbox.shape[1]
    subs = feats // piece_cols
    per_layer = layer // piece_cols
    outs = (att_ref, gt_ref, gs_ref)
    far = me + 2 * c - 1
    has_far = (far >= 0) & (far < seqs)

    def seq_of(zz, yy, cc):
        return (zz * chips_y + yy) * CORES + cc

    def slot(w, s):
        return wall_ref.at[w, pl.ds(pl.multiple_of(s * depth, depth), depth)]

    def send(w, s, src, sem, to):
        return pltpu.make_async_remote_copy(
            src_ref=src, dst_ref=slot(w, s), send_sem=sem, recv_sem=w_recv.at[w, s],
            device_id={"seq": to}, device_id_type=pl.DeviceIdType.MESH,
        )

    def arrived(w, s):
        send(w, s, slot(w, s), z_send.at[w, 0, 0], me).wait_recv()

    def up(w, zz, src):
        return send(w, seq_of(zz, y, c), src, z_send.at[w, zz, 0], me + chips_y * CORES)

    def down(w, zz, src):
        return send(w, seq_of(zz, y, c), src, z_send.at[w, zz, 1], me - chips_y * CORES)

    def across(w, zz, off, src):
        return send(
            w, seq_of(zz, y, c), src, y_send.at[w, zz, off],
            seq_of(z, lax.rem(y + off, chips_y), c),
        )

    def beside(w, zz, yy, src):
        return send(w, seq_of(zz, yy, c), src, c_send.at[w, zz, yy], seq_of(z, y, 1 - c))

    barrier = pltpu.get_barrier_semaphore()

    def greet(axis, to):
        pl.semaphore_signal(
            barrier, inc=1, device_id={axis: to}, device_id_type=pl.DeviceIdType.MESH
        )

    @pl.when(has_up)
    def _():
        greet("seq", me + chips_y * CORES)

    @pl.when(has_down)
    def _():
        greet("seq", me - chips_y * CORES)

    for off in range(1, chips_y):
        greet("seq", seq_of(z, lax.rem(y + off, chips_y), c))
    greet("seq", seq_of(z, y, 1 - c))

    @pl.when(has_far)
    def _():
        greet("seq", far)

    for off in range(1, heads):
        greet("head", lax.rem(hm + off, heads))
    pl.semaphore_wait(
        barrier,
        has_up.astype(jnp.int32)
        + has_down.astype(jnp.int32)
        + has_far.astype(jnp.int32)
        + (chips_y - 1 + 1 + heads - 1),
    )

    def act_copy(a, off):
        ref = (src_ref, tgt_ref, cot_ref)[a]
        return pltpu.make_async_remote_copy(
            src_ref=ref, dst_ref=acts.at[a, hm], send_sem=h_send.at[a, off],
            recv_sem=h_recv.at[a, hm], device_id={"head": lax.rem(hm + off, heads)},
            device_id_type=pl.DeviceIdType.MESH,
        )

    def act_arrived(a, off):
        came = lax.rem(hm + off, heads)
        pltpu.make_async_remote_copy(
            src_ref=acts.at[a, came], dst_ref=acts.at[a, came], send_sem=h_send.at[a, off],
            recv_sem=h_recv.at[a, came], device_id={"head": came},
            device_id_type=pl.DeviceIdType.MESH,
        ).wait_recv()

    def start_own(w):
        ref = own[w]

        @pl.when(has_up)
        def _():
            up(w, z, ref).start()

        @pl.when(has_down)
        def _():
            down(w, z, ref).start()

        for off in range(1, chips_y):
            across(w, z, off, ref).start()
        beside(w, z, y, ref).start()

    def relay_z(w, d):
        low, high = z - d, z + d

        @pl.when(low >= 0)
        def _():
            s = seq_of(low, y, c)
            arrived(w, s)

            @pl.when(has_up)
            def _():
                up(w, low, slot(w, s)).start()

            for off in range(1, chips_y):
                across(w, low, off, slot(w, s)).start()
            beside(w, low, y, slot(w, s)).start()

        @pl.when(high < CHIPS_Z)
        def _():
            s = seq_of(high, y, c)
            arrived(w, s)

            @pl.when(has_down)
            def _():
                down(w, high, slot(w, s)).start()

            for off in range(1, chips_y):
                across(w, high, off, slot(w, s)).start()
            beside(w, high, y, slot(w, s)).start()

    def relay_y(w, d):
        def one(zz):
            for off in range(1, chips_y):
                yy = lax.rem(y + off, chips_y)
                s = seq_of(zz, yy, c)
                arrived(w, s)
                beside(w, zz, yy, slot(w, s)).start()

        @pl.when(z - d >= 0)
        def _():
            one(z - d)

        if d > 0:

            @pl.when(z + d < CHIPS_Z)
            def _():
                one(z + d)

    def others(w):
        def one(i, carry):
            arrived(w, i * CORES + 1 - c)
            return carry

        lax.fori_loop(0, seqs // CORES, one, 0)

    def others_of_layer(w, zz):
        def one(yy, carry):
            arrived(w, seq_of(zz, yy, 1 - c))
            return carry

        lax.fori_loop(0, chips_y, one, 0)

    def project(w):
        tile = min(TILE, width)

        def columns(j, carry):
            cols = pl.ds(pl.multiple_of(j * tile, tile), tile)

            def part(h, total):
                return total + jnp.dot(
                    acts[ACT_OF[w], h],
                    wall_ref[w, pl.ds(pl.multiple_of(h * feats, feats), feats), cols],
                    preferred_element_type=jnp.float32,
                )

            total = lax.fori_loop(0, heads, part, jnp.zeros((rows, tile), jnp.float32))
            if w < 2:
                kvw[w, BLOCK : BLOCK + rows, cols] = total.astype(jnp.bfloat16)
            else:
                qd[w - 2, :, cols] = total.astype(jnp.bfloat16)
            return carry

        lax.fori_loop(0, width // tile, columns, 0)

    def halo_next(w):
        return pltpu.make_async_remote_copy(
            src_ref=kvw.at[w, pl.ds(rows, BLOCK)], dst_ref=kvw.at[w, pl.ds(0, BLOCK)],
            send_sem=f_send.at[w, 0], recv_sem=f_recv.at[w, 0],
            device_id={"seq": me + 1}, device_id_type=pl.DeviceIdType.MESH,
        )

    def halo_prev(w):
        return pltpu.make_async_remote_copy(
            src_ref=kvw.at[w, pl.ds(BLOCK, right)], dst_ref=kvw.at[w, pl.ds(BLOCK + rows, right)],
            send_sem=f_send.at[w, 1], recv_sem=f_recv.at[w, 1],
            device_id={"seq": me - 1}, device_id_type=pl.DeviceIdType.MESH,
        )

    def edge_next():
        return pltpu.make_async_remote_copy(
            src_ref=edge_out_high, dst_ref=edge_in_low, send_sem=b_send.at[0],
            recv_sem=b_recv.at[0], device_id={"seq": me + 1},
            device_id_type=pl.DeviceIdType.MESH,
        )

    def edge_prev():
        return pltpu.make_async_remote_copy(
            src_ref=edge_out_low, dst_ref=edge_in_high, send_sem=b_send.at[1],
            recv_sem=b_recv.at[1], device_id={"seq": me - 1},
            device_id_type=pl.DeviceIdType.MESH,
        )

    def halo_start(w):
        @pl.when(has_next)
        def _():
            halo_next(w).start()

        @pl.when(has_prev)
        def _():
            halo_prev(w).start()

    def halo_arrived():
        for w in range(2):

            @pl.when(has_prev)
            def _():
                halo_next(w).wait_recv()

            @pl.when(has_next)
            def _():
                halo_prev(w).wait_recv()

    def head_columns(h):
        return pl.ds(pl.multiple_of(h * HEAD_DIM, HEAD_DIM), HEAD_DIM)

    def dot_t(left, right_):
        return lax.dot_general(
            left, right_, (((1,), (1,)), ((), ())), preferred_element_type=jnp.float32
        )

    def dot_over_rows(left, right_):
        return lax.dot_general(
            left, right_, (((0,), (0,)), ((), ())), preferred_element_type=jnp.float32
        )

    def forward(h, carry):
        cols = head_columns(h)
        scores = dot_t(qd[0, :, cols], kvw[0, :, cols]) * scale + bias_ref[...]
        expo = jnp.exp(scores - jnp.max(scores, axis=1, keepdims=True))
        prob = expo * (1.0 / jnp.sum(expo, axis=1, keepdims=True))
        rounded = prob.astype(jnp.bfloat16)
        prob_ref[h] = prob
        probb_ref[h] = rounded
        ctx[:, cols] = jnp.dot(
            rounded, kvw[1, :, cols], preferred_element_type=jnp.float32
        ).astype(jnp.bfloat16)
        return carry

    def backward(h, carry):
        cols = head_columns(h)
        d_ctx = qd[1, :, cols]
        delta = jnp.sum(
            d_ctx.astype(jnp.float32) * ctx[:, cols].astype(jnp.float32), axis=1, keepdims=True
        )
        d_prob = dot_t(d_ctx, kvw[1, :, cols])
        d_score = (prob_ref[h] * (d_prob - delta) * scale).astype(jnp.bfloat16)
        dq[:, cols] = jnp.dot(
            d_score, kvw[0, :, cols], preferred_element_type=jnp.float32
        ).astype(jnp.bfloat16)
        dscore_ref[h] = d_score
        return carry

    def backward_source(h, carry):
        cols = head_columns(h)
        dkv[0, :, cols] = dot_over_rows(dscore_ref[h], qd[0, :, cols])
        dkv[1, :, cols] = dot_over_rows(probb_ref[h], qd[1, :, cols])
        return carry

    def out_copy(o, piece):
        to = piece // subs
        return pltpu.make_async_remote_copy(
            src_ref=outbox.at[o, piece], dst_ref=inbox.at[o, hm, lax.rem(piece, subs)],
            send_sem=o_send.at[o, piece], recv_sem=o_recv.at[o, hm, lax.rem(piece, subs)],
            device_id={"head": to}, device_id_type=pl.DeviceIdType.MESH,
        )

    def put_piece(o, piece):
        feat_rows = pl.ds(pl.multiple_of(piece * piece_cols, piece_cols), piece_cols)
        if o == 0:
            term = dot_t(ctx[...], wall_ref[3, feat_rows])
        elif o == 1:
            term = dot_t(dq[...], wall_ref[2, feat_rows])
        else:
            term = dot_t(dkvb[0], wall_ref[0, feat_rows]) + dot_t(dkvb[1], wall_ref[1, feat_rows])
        outbox[o, piece] = term.astype(jnp.bfloat16)

        @pl.when(piece // subs != hm)
        def _():
            out_copy(o, piece).start()

    def put_pieces(o, first, last):
        def one(i, carry):
            put_piece(o, lax.rem((hm + 1) * subs + i, pieces))
            return carry

        lax.fori_loop(first, last, one, 0)

    def finish(o):
        for sub in range(subs):
            total = outbox[o, hm * subs + sub].astype(jnp.float32)
            for off in range(1, heads):
                came = lax.rem(hm + off, heads)
                pltpu.make_async_remote_copy(
                    src_ref=inbox.at[o, came, sub], dst_ref=inbox.at[o, came, sub],
                    send_sem=o_send.at[o, 0], recv_sem=o_recv.at[o, came, sub],
                    device_id={"head": came}, device_id_type=pl.DeviceIdType.MESH,
                ).wait_recv()
                total = total + inbox[o, came, sub].astype(jnp.float32)
            outs[o][:, sub * piece_cols : (sub + 1) * piece_cols] = total.astype(jnp.bfloat16)

    def own_copy(w):
        return pltpu.make_async_copy(own[w], slot(w, me), own_sem.at[w])

    def own_act(a):
        ref = (src_ref, tgt_ref, cot_ref)[a]
        return pltpu.make_async_copy(ref, acts.at[a, hm], own_sem.at[4 + a])

    start_own(0)
    for off in range(1, heads):
        act_copy(0, off).start()
    for a in (1, 2):
        for off in range(1, heads):
            act_copy(a, off).start()
    for w in range(4):
        own_copy(w).start()
    for a in range(3):
        own_act(a).start()
    kvw[:, BLOCK + rows + right :] = jnp.zeros_like(kvw[:, BLOCK + rows + right :])

    @pl.when(me == 0)
    def _():
        kvw[:, :BLOCK] = jnp.zeros_like(kvw[:, :BLOCK])
        edge_in_low[...] = jnp.zeros_like(edge_in_low)

    @pl.when(me == seqs - 1)
    def _():
        kvw[:, BLOCK + rows : BLOCK + rows + right] = jnp.zeros_like(
            kvw[:, BLOCK + rows : BLOCK + rows + right]
        )
        edge_in_high[...] = jnp.zeros_like(edge_in_high)

    def acts_ready(a):
        own_act(a).wait()
        for off in range(1, heads):
            act_arrived(a, off)

    def complete(w, first):
        if first:
            acts_ready(ACT_OF[w])
        own_copy(w).wait()
        others(w)
        project(w)

    def attended_layer(zz):
        others_of_layer(3, zz)

        def one(j, carry):
            put_piece(0, zz * per_layer + j)
            return carry

        lax.fori_loop(0, per_layer, one, 0)

    def attended_at(d):
        @pl.when(z - d >= 0)
        def _():
            attended_layer(z - d)

        if d > 0:

            @pl.when(z + d < CHIPS_Z)
            def _():
                attended_layer(z + d)

    z_steps = [(w, d) for w in range(4) for d in range(1, CHIPS_Z)]
    y_steps = [(w, d) for w in range(4) for d in range(CHIPS_Z)]
    for i in range(len(y_steps)):
        if i < len(z_steps):
            w, d = z_steps[i]
            relay_z(w, d)
            if d == 1 and w + 1 < 4:
                start_own(w + 1)
        w, d = y_steps[i]
        relay_y(w, d)
        if w == 3:
            if d == 0:
                own_copy(3).wait()
            attended_at(d)
        elif d == CHIPS_Z - 1:
            complete(w, ACT_OF[w] not in ACT_OF[:w])
            if w < 2:
                halo_start(w)
            else:
                halo_arrived()
                lax.fori_loop(0, local_heads, forward, 0)
    acts_ready(2)
    project(3)
    lax.fori_loop(0, local_heads, backward, 0)
    put_pieces(1, 0, pieces - subs)
    lax.fori_loop(0, local_heads, backward_source, 0)
    edge_out_low[...] = dkv[:, :BLOCK].astype(jnp.bfloat16)
    edge_out_high[...] = dkv[:, BLOCK + rows : BLOCK + rows + right].astype(jnp.bfloat16)

    @pl.when(has_next)
    def _():
        edge_next().start()

    @pl.when(has_prev)
    def _():
        edge_prev().start()

    put_pieces(1, pieces - subs, pieces)

    @pl.when(has_prev)
    def _():
        edge_next().wait_recv()

    @pl.when(has_next)
    def _():
        edge_prev().wait_recv()

    middle = rows - BLOCK
    dkvb[:, :right] = (
        dkv[:, BLOCK : BLOCK + right] + edge_in_low[...].astype(jnp.float32)
    ).astype(jnp.bfloat16)
    if middle > right:
        dkvb[:, right:middle] = dkv[:, BLOCK + right : BLOCK + middle].astype(jnp.bfloat16)
    dkvb[:, middle:] = (
        dkv[:, BLOCK + middle : BLOCK + rows] + edge_in_high[...].astype(jnp.float32)
    ).astype(jnp.bfloat16)
    put_pieces(2, 0, pieces)
    for o in range(3):
        finish(o)

    def drain(w):
        for zz in range(CHIPS_Z):

            @pl.when(has_up & (zz <= z))
            def _():
                up(w, zz, own[0]).wait_send()

            @pl.when(has_down & (zz >= z))
            def _():
                down(w, zz, own[0]).wait_send()

            for off in range(1, chips_y):
                across(w, zz, off, own[0]).wait_send()

            def side(yy, carry):
                beside(w, zz, yy, own[0]).wait_send()
                return carry

            lax.fori_loop(0, chips_y, side, 0)

    for w in range(4):
        drain(w)
    for a in range(3):
        for off in range(1, heads):
            act_copy(a, off).wait_send()

    def out_drain(o, piece):
        @pl.when(piece // subs != hm)
        def _():
            out_copy(o, piece).wait_send()

    for o in range(3):
        for piece in range(pieces):
            out_drain(o, piece)

    @pl.when(has_next)
    def _():
        edge_next().wait_send()
        for w in range(2):
            halo_next(w).wait_send()

    @pl.when(has_prev)
    def _():
        edge_prev().wait_send()
        for w in range(2):
            halo_prev(w).wait_send()


def sublayer(seqs, heads, target, source, cotangent, wk, wv, wq, wo, bias):
    rows, feats = target.shape
    depth, width = wk.shape
    span = bias.shape[1]
    local_heads = width // HEAD_DIM
    right = (MAXW - 1) * BLOCK
    chips_y = seqs // (CHIPS_Z * CORES)
    piece_cols = min(feats, seqs * depth // CHIPS_Z)
    pieces = seqs * depth // piece_cols
    subs = feats // piece_cols
    vmem = pl.BlockSpec(memory_space=pltpu.VMEM)
    hbm = pl.BlockSpec(memory_space=pl.ANY)
    half, fone = jnp.bfloat16, jnp.float32
    return pl.pallas_call(
        functools.partial(sublayer_kernel, seqs, heads),
        out_shape=(jax.ShapeDtypeStruct((rows, feats), half),) * 3,
        in_specs=[hbm] * 7 + [vmem],
        out_specs=(vmem,) * 3,
        scratch_shapes=[
            pltpu.VMEM((4, seqs * depth, width), half),
            pltpu.VMEM((3, heads, rows, feats), half),
            pltpu.VMEM((2, span, width), half),
            pltpu.VMEM((2, rows, width), half),
            pltpu.VMEM((local_heads, rows, span), fone),
            pltpu.VMEM((local_heads, rows, span), half),
            pltpu.VMEM((local_heads, rows, span), half),
            pltpu.VMEM((rows, width), half),
            pltpu.VMEM((rows, width), half),
            pltpu.VMEM((2, span, width), fone),
            pltpu.VMEM((2, rows, width), half),
            pltpu.VMEM((2, BLOCK, width), half),
            pltpu.VMEM((2, right, width), half),
            pltpu.VMEM((2, right, width), half),
            pltpu.VMEM((2, BLOCK, width), half),
            pltpu.VMEM((3, pieces, rows, piece_cols), half),
            pltpu.VMEM((3, heads, subs, rows, piece_cols), half),
            pltpu.SemaphoreType.DMA((4, CHIPS_Z, 2)),
            pltpu.SemaphoreType.DMA((4, CHIPS_Z, chips_y)),
            pltpu.SemaphoreType.DMA((4, CHIPS_Z, chips_y)),
            pltpu.SemaphoreType.DMA((4, seqs)),
            pltpu.SemaphoreType.DMA((3, heads)),
            pltpu.SemaphoreType.DMA((3, heads)),
            pltpu.SemaphoreType.DMA((7,)),
            pltpu.SemaphoreType.DMA((2, 2)),
            pltpu.SemaphoreType.DMA((2, 2)),
            pltpu.SemaphoreType.DMA((2,)),
            pltpu.SemaphoreType.DMA((2,)),
            pltpu.SemaphoreType.DMA((3, pieces)),
            pltpu.SemaphoreType.DMA((3, heads, subs)),
        ],
        compiler_params=pltpu.CompilerParams(
            collective_id=0, has_side_effects=True, vmem_limit_bytes=56 * 1024 * 1024
        ),
        cost_estimate=pl.CostEstimate(
            flops=16 * rows * seqs * depth * width,
            bytes_accessed=8 * seqs * depth * width,
            transcendentals=local_heads * rows * span,
        ),
    )(source, target, cotangent, wk, wv, wq, wo, bias)


def per_device(target, source, w_query, w_key, w_value, w_out, band_start, band_end, cotangent):
    rows = target.shape[0]
    blocks = rows // BLOCK
    span = -(-(rows + MAXW * BLOCK) // 128) * 128
    anchor = lax.axis_index("seq") * blocks - 1
    low_rows = jnp.repeat(band_start - anchor, BLOCK)[:, None]
    high_rows = jnp.repeat(band_end - anchor, BLOCK)[:, None]
    key_block = (jnp.arange(span, dtype=jnp.int32) // BLOCK)[None, :]
    visible = (key_block >= low_rows) & (key_block < high_rows)
    bias = jnp.where(visible, 0.0, -jnp.inf).astype(jnp.float32)
    return sublayer(
        lax.axis_size("seq"), lax.axis_size("head"),
        target, source, cotangent, w_key, w_value, w_query, w_out, bias,
    )


def solution(mesh):
    both = P("seq", "head")
    return jax.shard_map(
        per_device,
        mesh=mesh,
        in_specs=(both,) * 6 + (P("seq"), P("seq"), both),
        out_specs=(both,) * 3,
        check_vma=False,
    )
```

```python
import functools

import jax
import jax.numpy as jnp
from jax import lax
from jax.experimental import pallas as pl
from jax.experimental.pallas import tpu as pltpu
from jax.sharding import PartitionSpec as P

HEAD_DIM = 128
BLOCK = 64
MAXW = 3
CHIPS_Z = 4
CORES = 2
ACT_OF = (0, 0, 1, 2)
TILE = 256


def lead_rows(depth):
    return max(16, depth // 8)


def sublayer_kernel(
    seqs, heads, src_ref, tgt_ref, cot_ref, wk_ref, wv_ref, wq_ref, wo_ref, bias_ref,
    att_ref, gt_ref, gs_ref,
    wall_ref, acts, kvw, qd, prob_ref, probb_ref, dscore_ref, ctx, dq, dkv, dkvb,
    edge_out_low, edge_out_high, edge_in_low, edge_in_high, outbox, inbox,
    z_send, l_send, y_send, k_send, c_send, w_recv, h_send, h_recv, own_sem,
    f_send, f_recv, b_send, b_recv, o_send, o_recv,
):
    chips_y = seqs // (CHIPS_Z * CORES)
    me = lax.axis_index("seq")
    hm = lax.axis_index("head")
    z = me // (chips_y * CORES)
    y = lax.rem(me // CORES, chips_y)
    c = lax.rem(me, CORES)
    own = (wk_ref, wv_ref, wq_ref, wo_ref)
    depth = wk_ref.shape[0]
    rows = src_ref.shape[0]
    feats = src_ref.shape[1]
    width = wk_ref.shape[1]
    has_up = z < CHIPS_Z - 1
    has_down = z > 0
    has_next = me < seqs - 1
    has_prev = me > 0
    span = kvw.shape[1]
    right = (MAXW - 1) * BLOCK
    local_heads = width // HEAD_DIM
    scale = HEAD_DIM ** (-0.5)
    layer = seqs * depth // CHIPS_Z
    piece_cols = outbox.shape[3]
    pieces = outbox.shape[1]
    subs = feats // piece_cols
    per_layer = layer // piece_cols
    outs = (att_ref, gt_ref, gs_ref)
    far = me + 2 * c - 1
    has_far = (far >= 0) & (far < seqs)

    def seq_of(zz, yy, cc):
        return (zz * chips_y + yy) * CORES + cc

    lead = lead_rows(depth)
    begin = (0, lead)
    size = (lead, depth - lead)

    def slot(w, s):
        return wall_ref.at[w, pl.ds(pl.multiple_of(s * depth, depth), depth)]

    def part(w, s, p):
        return wall_ref.at[w, pl.ds(pl.multiple_of(s * depth + begin[p], 16), size[p])]

    def own_part(w, p):
        return own[w].at[pl.ds(begin[p], size[p])]

    def send(src, dst, send_sem, recv_sem, to):
        return pltpu.make_async_remote_copy(
            src_ref=src, dst_ref=dst, send_sem=send_sem, recv_sem=recv_sem,
            device_id={"seq": to}, device_id_type=pl.DeviceIdType.MESH,
        )

    def arrived(w, s, p):
        send(part(w, s, p), part(w, s, p), z_send.at[w, 0, 0], w_recv.at[w, s, p], me).wait_recv()

    def arrived_beside(w, s):
        send(slot(w, s), slot(w, s), z_send.at[w, 0, 0], w_recv.at[w, s, 0], me).wait_recv()

    def along(w, zz, yy, p, src, step):
        s = seq_of(zz, yy, c)
        which = (step + 1) // 2
        sem = z_send.at[w, zz, which] if p else l_send.at[w, zz, which, yy]
        return send(src, part(w, s, p), sem, w_recv.at[w, s, p], me + step * chips_y * CORES)

    def across(w, zz, off, p, src):
        s = seq_of(zz, y, c)
        sem = y_send.at[w, zz, off] if p else k_send.at[w, off]
        return send(
            src, part(w, s, p), sem, w_recv.at[w, s, p], seq_of(z, lax.rem(y + off, chips_y), c)
        )

    def beside(w, zz, yy, src, dst):
        s = seq_of(zz, yy, c)
        return send(src, dst, c_send.at[w, zz, yy], w_recv.at[w, s, 0], seq_of(z, y, 1 - c))

    def beside_part(w, zz, yy, p):
        s = seq_of(zz, yy, c)
        beside(w, zz, yy, part(w, s, p), part(w, s, p)).start()

    barrier = pltpu.get_barrier_semaphore()

    def greet(axis, to):
        pl.semaphore_signal(
            barrier, inc=1, device_id={axis: to}, device_id_type=pl.DeviceIdType.MESH
        )

    @pl.when(has_up)
    def _():
        greet("seq", me + chips_y * CORES)

    @pl.when(has_down)
    def _():
        greet("seq", me - chips_y * CORES)

    for off in range(1, chips_y):
        greet("seq", seq_of(z, lax.rem(y + off, chips_y), c))
    greet("seq", seq_of(z, y, 1 - c))

    @pl.when(has_far)
    def _():
        greet("seq", far)

    for off in range(1, heads):
        greet("head", lax.rem(hm + off, heads))
    pl.semaphore_wait(
        barrier,
        has_up.astype(jnp.int32)
        + has_down.astype(jnp.int32)
        + has_far.astype(jnp.int32)
        + (chips_y - 1 + 1 + heads - 1),
    )

    def act_copy(a, off):
        ref = (src_ref, tgt_ref, cot_ref)[a]
        return pltpu.make_async_remote_copy(
            src_ref=ref, dst_ref=acts.at[a, hm], send_sem=h_send.at[a, off],
            recv_sem=h_recv.at[a, hm], device_id={"head": lax.rem(hm + off, heads)},
            device_id_type=pl.DeviceIdType.MESH,
        )

    def act_arrived(a, off):
        came = lax.rem(hm + off, heads)
        pltpu.make_async_remote_copy(
            src_ref=acts.at[a, came], dst_ref=acts.at[a, came], send_sem=h_send.at[a, off],
            recv_sem=h_recv.at[a, came], device_id={"head": came},
            device_id_type=pl.DeviceIdType.MESH,
        ).wait_recv()

    def start_own(w):
        for p in range(2):
            for off in range(1, chips_y):
                across(w, z, off, p, own_part(w, p)).start()
            onward(w, z, y, p, own_part(w, p), True, True)
        beside(w, z, y, own[w], slot(w, me)).start()

    def onward(w, zz, yy, p, src, upward, downward):
        if upward:

            @pl.when(has_up)
            def _():
                along(w, zz, yy, p, src, 1).start()

        if downward:

            @pl.when(has_down)
            def _():
                along(w, zz, yy, p, src, -1).start()

    def relay_lead(w):
        for off in range(1, chips_y):
            yy = lax.rem(y + off, chips_y)
            s = seq_of(z, yy, c)
            arrived(w, s, 0)
            onward(w, z, yy, 0, part(w, s, 0), True, True)
            beside_part(w, z, yy, 0)

    def relay_z(w, d):
        def one(zz, upward):
            s = seq_of(zz, y, c)
            arrived(w, s, 1)
            for off in range(1, chips_y):
                across(w, zz, off, 1, part(w, s, 1)).start()
            onward(w, zz, y, 1, part(w, s, 1), upward, not upward)
            beside_part(w, zz, y, 1)

            def ahead(yy, carry):
                sl = seq_of(zz, yy, c)
                arrived(w, sl, 0)
                onward(w, zz, yy, 0, part(w, sl, 0), upward, not upward)
                beside_part(w, zz, yy, 0)
                return carry

            lax.fori_loop(0, chips_y, ahead, 0)

        @pl.when(z - d >= 0)
        def _():
            one(z - d, True)

        @pl.when(z + d < CHIPS_Z)
        def _():
            one(z + d, False)

    def relay_y(w, d):
        def one(zz):
            for off in range(1, chips_y):
                yy = lax.rem(y + off, chips_y)
                arrived(w, seq_of(zz, yy, c), 1)
                beside_part(w, zz, yy, 1)

        @pl.when(z - d >= 0)
        def _():
            one(z - d)

        if d > 0:

            @pl.when(z + d < CHIPS_Z)
            def _():
                one(z + d)

    def others(w):
        def one(i, carry):
            arrived_beside(w, i * CORES + 1 - c)
            return carry

        lax.fori_loop(0, seqs // CORES, one, 0)

    def others_of_layer(w, zz):
        def one(yy, carry):
            arrived_beside(w, seq_of(zz, yy, 1 - c))
            return carry

        lax.fori_loop(0, chips_y, one, 0)

    def project(w):
        tile = min(TILE, width)

        def columns(j, carry):
            cols = pl.ds(pl.multiple_of(j * tile, tile), tile)

            def block(h, total):
                return total + jnp.dot(
                    acts[ACT_OF[w], h],
                    wall_ref[w, pl.ds(pl.multiple_of(h * feats, feats), feats), cols],
                    preferred_element_type=jnp.float32,
                )

            total = lax.fori_loop(0, heads, block, jnp.zeros((rows, tile), jnp.float32))
            if w < 2:
                kvw[w, BLOCK : BLOCK + rows, cols] = total.astype(jnp.bfloat16)
            else:
                qd[w - 2, :, cols] = total.astype(jnp.bfloat16)
            return carry

        lax.fori_loop(0, width // tile, columns, 0)

    def halo_next(w):
        return pltpu.make_async_remote_copy(
            src_ref=kvw.at[w, pl.ds(rows, BLOCK)], dst_ref=kvw.at[w, pl.ds(0, BLOCK)],
            send_sem=f_send.at[w, 0], recv_sem=f_recv.at[w, 0],
            device_id={"seq": me + 1}, device_id_type=pl.DeviceIdType.MESH,
        )

    def halo_prev(w):
        return pltpu.make_async_remote_copy(
            src_ref=kvw.at[w, pl.ds(BLOCK, right)], dst_ref=kvw.at[w, pl.ds(BLOCK + rows, right)],
            send_sem=f_send.at[w, 1], recv_sem=f_recv.at[w, 1],
            device_id={"seq": me - 1}, device_id_type=pl.DeviceIdType.MESH,
        )

    def edge_next():
        return pltpu.make_async_remote_copy(
            src_ref=edge_out_high, dst_ref=edge_in_low, send_sem=b_send.at[0],
            recv_sem=b_recv.at[0], device_id={"seq": me + 1},
            device_id_type=pl.DeviceIdType.MESH,
        )

    def edge_prev():
        return pltpu.make_async_remote_copy(
            src_ref=edge_out_low, dst_ref=edge_in_high, send_sem=b_send.at[1],
            recv_sem=b_recv.at[1], device_id={"seq": me - 1},
            device_id_type=pl.DeviceIdType.MESH,
        )

    def halo_start(w):
        @pl.when(has_next)
        def _():
            halo_next(w).start()

        @pl.when(has_prev)
        def _():
            halo_prev(w).start()

    def halo_arrived():
        for w in range(2):

            @pl.when(has_prev)
            def _():
                halo_next(w).wait_recv()

            @pl.when(has_next)
            def _():
                halo_prev(w).wait_recv()

    def head_columns(h):
        return pl.ds(pl.multiple_of(h * HEAD_DIM, HEAD_DIM), HEAD_DIM)

    def dot_t(left, right_):
        return lax.dot_general(
            left, right_, (((1,), (1,)), ((), ())), preferred_element_type=jnp.float32
        )

    def dot_over_rows(left, right_):
        return lax.dot_general(
            left, right_, (((0,), (0,)), ((), ())), preferred_element_type=jnp.float32
        )

    def forward(h, carry):
        cols = head_columns(h)
        scores = dot_t(qd[0, :, cols], kvw[0, :, cols]) * scale + bias_ref[...]
        expo = jnp.exp(scores - jnp.max(scores, axis=1, keepdims=True))
        prob = expo * (1.0 / jnp.sum(expo, axis=1, keepdims=True))
        rounded = prob.astype(jnp.bfloat16)
        prob_ref[h] = prob
        probb_ref[h] = rounded
        ctx[:, cols] = jnp.dot(
            rounded, kvw[1, :, cols], preferred_element_type=jnp.float32
        ).astype(jnp.bfloat16)
        return carry

    def backward(h, carry):
        cols = head_columns(h)
        d_ctx = qd[1, :, cols]
        delta = jnp.sum(
            d_ctx.astype(jnp.float32) * ctx[:, cols].astype(jnp.float32), axis=1, keepdims=True
        )
        d_prob = dot_t(d_ctx, kvw[1, :, cols])
        d_score = (prob_ref[h] * (d_prob - delta) * scale).astype(jnp.bfloat16)
        dq[:, cols] = jnp.dot(
            d_score, kvw[0, :, cols], preferred_element_type=jnp.float32
        ).astype(jnp.bfloat16)
        dscore_ref[h] = d_score
        return carry

    def backward_source(h, carry):
        cols = head_columns(h)
        dkv[0, :, cols] = dot_over_rows(dscore_ref[h], qd[0, :, cols])
        dkv[1, :, cols] = dot_over_rows(probb_ref[h], qd[1, :, cols])
        return carry

    def out_copy(o, piece):
        to = piece // subs
        return pltpu.make_async_remote_copy(
            src_ref=outbox.at[o, piece], dst_ref=inbox.at[o, hm, lax.rem(piece, subs)],
            send_sem=o_send.at[o, piece], recv_sem=o_recv.at[o, hm, lax.rem(piece, subs)],
            device_id={"head": to}, device_id_type=pl.DeviceIdType.MESH,
        )

    def put_piece(o, piece):
        feat_rows = pl.ds(pl.multiple_of(piece * piece_cols, piece_cols), piece_cols)
        if o == 0:
            term = dot_t(ctx[...], wall_ref[3, feat_rows])
        elif o == 1:
            term = dot_t(dq[...], wall_ref[2, feat_rows])
        else:
            term = dot_t(dkvb[0], wall_ref[0, feat_rows]) + dot_t(dkvb[1], wall_ref[1, feat_rows])
        outbox[o, piece] = term.astype(jnp.bfloat16)

        @pl.when(piece // subs != hm)
        def _():
            out_copy(o, piece).start()

    def put_pieces(o, first, last):
        def one(i, carry):
            put_piece(o, lax.rem((hm + 1) * subs + i, pieces))
            return carry

        lax.fori_loop(first, last, one, 0)

    def finish(o):
        for sub in range(subs):
            total = outbox[o, hm * subs + sub].astype(jnp.float32)
            for off in range(1, heads):
                came = lax.rem(hm + off, heads)
                pltpu.make_async_remote_copy(
                    src_ref=inbox.at[o, came, sub], dst_ref=inbox.at[o, came, sub],
                    send_sem=o_send.at[o, 0], recv_sem=o_recv.at[o, came, sub],
                    device_id={"head": came}, device_id_type=pl.DeviceIdType.MESH,
                ).wait_recv()
                total = total + inbox[o, came, sub].astype(jnp.float32)
            outs[o][:, sub * piece_cols : (sub + 1) * piece_cols] = total.astype(jnp.bfloat16)

    def own_copy(w):
        return pltpu.make_async_copy(own[w], slot(w, me), own_sem.at[w])

    def own_act(a):
        ref = (src_ref, tgt_ref, cot_ref)[a]
        return pltpu.make_async_copy(ref, acts.at[a, hm], own_sem.at[4 + a])

    start_own(0)
    for off in range(1, heads):
        act_copy(0, off).start()
    for a in (1, 2):
        for off in range(1, heads):
            act_copy(a, off).start()
    for w in range(4):
        own_copy(w).start()
    for a in range(3):
        own_act(a).start()
    kvw[:, BLOCK + rows + right :] = jnp.zeros_like(kvw[:, BLOCK + rows + right :])

    @pl.when(me == 0)
    def _():
        kvw[:, :BLOCK] = jnp.zeros_like(kvw[:, :BLOCK])
        edge_in_low[...] = jnp.zeros_like(edge_in_low)

    @pl.when(me == seqs - 1)
    def _():
        kvw[:, BLOCK + rows : BLOCK + rows + right] = jnp.zeros_like(
            kvw[:, BLOCK + rows : BLOCK + rows + right]
        )
        edge_in_high[...] = jnp.zeros_like(edge_in_high)

    def acts_ready(a):
        own_act(a).wait()
        for off in range(1, heads):
            act_arrived(a, off)

    def complete(w, first):
        if first:
            acts_ready(ACT_OF[w])
        own_copy(w).wait()
        others(w)
        project(w)

    def attended_layer(zz):
        others_of_layer(3, zz)

        def one(j, carry):
            put_piece(0, zz * per_layer + j)
            return carry

        lax.fori_loop(0, per_layer, one, 0)

    def attended_at(d):
        @pl.when(z - d >= 0)
        def _():
            attended_layer(z - d)

        if d > 0:

            @pl.when(z + d < CHIPS_Z)
            def _():
                attended_layer(z + d)

    z_steps = [(w, d) for w in range(4) for d in range(1, CHIPS_Z)]
    y_steps = [(w, d) for w in range(4) for d in range(CHIPS_Z)]
    for i in range(len(y_steps)):
        if i < len(z_steps):
            w, d = z_steps[i]
            if d == 1:
                relay_lead(w)
            relay_z(w, d)
            if d == 1 and w + 1 < 4:
                start_own(w + 1)
        w, d = y_steps[i]
        relay_y(w, d)
        if w == 3:
            if d == 0:
                own_copy(3).wait()
            attended_at(d)
        elif d == CHIPS_Z - 1:
            complete(w, ACT_OF[w] not in ACT_OF[:w])
            if w < 2:
                halo_start(w)
            else:
                halo_arrived()
                lax.fori_loop(0, local_heads, forward, 0)
    acts_ready(2)
    project(3)
    lax.fori_loop(0, local_heads, backward, 0)
    put_pieces(1, 0, pieces - subs)
    lax.fori_loop(0, local_heads, backward_source, 0)
    edge_out_low[...] = dkv[:, :BLOCK].astype(jnp.bfloat16)
    edge_out_high[...] = dkv[:, BLOCK + rows : BLOCK + rows + right].astype(jnp.bfloat16)

    @pl.when(has_next)
    def _():
        edge_next().start()

    @pl.when(has_prev)
    def _():
        edge_prev().start()

    put_pieces(1, pieces - subs, pieces)

    @pl.when(has_prev)
    def _():
        edge_next().wait_recv()

    @pl.when(has_next)
    def _():
        edge_prev().wait_recv()

    middle = rows - BLOCK
    dkvb[:, :right] = (
        dkv[:, BLOCK : BLOCK + right] + edge_in_low[...].astype(jnp.float32)
    ).astype(jnp.bfloat16)
    if middle > right:
        dkvb[:, right:middle] = dkv[:, BLOCK + right : BLOCK + middle].astype(jnp.bfloat16)
    dkvb[:, middle:] = (
        dkv[:, BLOCK + middle : BLOCK + rows] + edge_in_high[...].astype(jnp.float32)
    ).astype(jnp.bfloat16)
    put_pieces(2, 0, pieces)
    for o in range(3):
        finish(o)

    def drain(w):
        for zz in range(CHIPS_Z):

            @pl.when(has_up & (zz <= z))
            def _():
                along(w, zz, y, 1, own_part(w, 1), 1).wait_send()

            @pl.when(has_down & (zz >= z))
            def _():
                along(w, zz, y, 1, own_part(w, 1), -1).wait_send()

            for off in range(1, chips_y):
                across(w, zz, off, 1, own_part(w, 1)).wait_send()

            def side(yy, carry):
                beside(w, zz, yy, own[w], slot(w, me)).wait_send()

                @pl.when(has_up & (zz <= z))
                def _():
                    along(w, zz, yy, 0, own_part(w, 0), 1).wait_send()

                @pl.when(has_down & (zz >= z))
                def _():
                    along(w, zz, yy, 0, own_part(w, 0), -1).wait_send()

                return carry

            lax.fori_loop(0, chips_y, side, 0)
        for off in range(1, chips_y):
            across(w, z, off, 0, own_part(w, 0)).wait_send()

    for w in range(4):
        drain(w)
    for a in range(3):
        for off in range(1, heads):
            act_copy(a, off).wait_send()

    def out_drain(o, piece):
        @pl.when(piece // subs != hm)
        def _():
            out_copy(o, piece).wait_send()

    for o in range(3):
        for piece in range(pieces):
            out_drain(o, piece)

    @pl.when(has_next)
    def _():
        edge_next().wait_send()
        for w in range(2):
            halo_next(w).wait_send()

    @pl.when(has_prev)
    def _():
        edge_prev().wait_send()
        for w in range(2):
            halo_prev(w).wait_send()


def sublayer(seqs, heads, target, source, cotangent, wk, wv, wq, wo, bias):
    rows, feats = target.shape
    depth, width = wk.shape
    span = bias.shape[1]
    local_heads = width // HEAD_DIM
    right = (MAXW - 1) * BLOCK
    chips_y = seqs // (CHIPS_Z * CORES)
    piece_cols = min(feats, seqs * depth // CHIPS_Z)
    pieces = seqs * depth // piece_cols
    subs = feats // piece_cols
    vmem = pl.BlockSpec(memory_space=pltpu.VMEM)
    hbm = pl.BlockSpec(memory_space=pl.ANY)
    half, fone = jnp.bfloat16, jnp.float32
    return pl.pallas_call(
        functools.partial(sublayer_kernel, seqs, heads),
        out_shape=(jax.ShapeDtypeStruct((rows, feats), half),) * 3,
        in_specs=[hbm] * 7 + [vmem],
        out_specs=(vmem,) * 3,
        scratch_shapes=[
            pltpu.VMEM((4, seqs * depth, width), half),
            pltpu.VMEM((3, heads, rows, feats), half),
            pltpu.VMEM((2, span, width), half),
            pltpu.VMEM((2, rows, width), half),
            pltpu.VMEM((local_heads, rows, span), fone),
            pltpu.VMEM((local_heads, rows, span), half),
            pltpu.VMEM((local_heads, rows, span), half),
            pltpu.VMEM((rows, width), half),
            pltpu.VMEM((rows, width), half),
            pltpu.VMEM((2, span, width), fone),
            pltpu.VMEM((2, rows, width), half),
            pltpu.VMEM((2, BLOCK, width), half),
            pltpu.VMEM((2, right, width), half),
            pltpu.VMEM((2, right, width), half),
            pltpu.VMEM((2, BLOCK, width), half),
            pltpu.VMEM((3, pieces, rows, piece_cols), half),
            pltpu.VMEM((3, heads, subs, rows, piece_cols), half),
            pltpu.SemaphoreType.DMA((4, CHIPS_Z, 2)),
            pltpu.SemaphoreType.DMA((4, CHIPS_Z, 2, chips_y)),
            pltpu.SemaphoreType.DMA((4, CHIPS_Z, chips_y)),
            pltpu.SemaphoreType.DMA((4, chips_y)),
            pltpu.SemaphoreType.DMA((4, CHIPS_Z, chips_y)),
            pltpu.SemaphoreType.DMA((4, seqs, 2)),
            pltpu.SemaphoreType.DMA((3, heads)),
            pltpu.SemaphoreType.DMA((3, heads)),
            pltpu.SemaphoreType.DMA((7,)),
            pltpu.SemaphoreType.DMA((2, 2)),
            pltpu.SemaphoreType.DMA((2, 2)),
            pltpu.SemaphoreType.DMA((2,)),
            pltpu.SemaphoreType.DMA((2,)),
            pltpu.SemaphoreType.DMA((3, pieces)),
            pltpu.SemaphoreType.DMA((3, heads, subs)),
        ],
        compiler_params=pltpu.CompilerParams(
            collective_id=0, has_side_effects=True, vmem_limit_bytes=56 * 1024 * 1024
        ),
        cost_estimate=pl.CostEstimate(
            flops=16 * rows * seqs * depth * width,
            bytes_accessed=8 * seqs * depth * width,
            transcendentals=local_heads * rows * span,
        ),
    )(source, target, cotangent, wk, wv, wq, wo, bias)


def per_device(target, source, w_query, w_key, w_value, w_out, band_start, band_end, cotangent):
    rows = target.shape[0]
    blocks = rows // BLOCK
    span = -(-(rows + MAXW * BLOCK) // 128) * 128
    anchor = lax.axis_index("seq") * blocks - 1
    low_rows = jnp.repeat(band_start - anchor, BLOCK)[:, None]
    high_rows = jnp.repeat(band_end - anchor, BLOCK)[:, None]
    key_block = (jnp.arange(span, dtype=jnp.int32) // BLOCK)[None, :]
    visible = (key_block >= low_rows) & (key_block < high_rows)
    bias = jnp.where(visible, 0.0, -jnp.inf).astype(jnp.float32)
    return sublayer(
        lax.axis_size("seq"), lax.axis_size("head"),
        target, source, cotangent, w_key, w_value, w_query, w_out, bias,
    )


def solution(mesh):
    both = P("seq", "head")
    return jax.shard_map(
        per_device,
        mesh=mesh,
        in_specs=(both,) * 6 + (P("seq"), P("seq"), both),
        out_specs=(both,) * 3,
        check_vma=False,
    )
```
